32 devices in a mesh: wl: 2 (over y), gz: 16 (over z, x, core).
Axes of the slice: x: 2, y: 2, z: 4, core: 2. Of those that a mesh axis runs over, the one named last changes fastest.
Arguments:
- labels: int32 [128, 128, 128], P('gz'), may hold values from 0 to 7
- label_table: float32 [8, 5], replicated, may hold values from 0.1 to 1.5
- spectra: float32 [32, 6], P('wl'), may hold values from 0.2 to 2
- illumination: int32 [128, 128], replicated, may hold values 0 or 1
- fluence_start: float32 [32, 128, 128, 128], P('wl', 'gz'), as said below
- measured: float32 [32, 128, 128, 128], P('wl', 'gz'), may hold values from 0 to 2
Outputs:
- fluence: float32 [32, 128, 128, 128], P('wl', 'gz')
- concentrations: float32 [4, 128, 128, 128], P(None, 'gz')
- scattering: float32 [128, 128, 128], P('gz')
The draws below stay inside these ranges and needn't reach their ends.
Inputs may be any that keep to these rules, and one draw needn't show every extreme that they name: `fluence_start`: positive, of order one.
All inputs are finite; a program needn't handle non-finite values.
Results may differ from the reference program's by a relative error of at most 0.0003.
Values sent between devices are 32-bit elements; how exact they have to be, the bound alone decides.
A program may use at most 192 MiB of HBM per device.

```python
import math
import jax
import jax.numpy as jnp
from jax import lax

WAVES = 32
CHROMO = 4
LABELS = 8
ITERS = 2
NY = 128
NX = 128
NZ = 128
CELLS = 2097152


def draw_fluence_start(key, part):
    key = jax.random.fold_in(key, 11)
    depth = jnp.arange(NZ, dtype=jnp.float32) / max(NZ - 1, 1)
    shape = (WAVES, NZ, NY, NX)
    rough = jnp.exp(jax.random.uniform(key, shape, jnp.float32, math.log(0.3), math.log(3.0)))
    decay = jnp.exp(-math.log(3.0) * depth)
    return rough * decay[None, :, None, None]


def set_ends(entries, own_key, low, high):
    longest = entries.shape.index(max(entries.shape))
    spots = []
    for shift in (0, 1):
        where = [jax.random.randint(jax.random.fold_in(own_key, axis), (), 0, length) for axis, length in enumerate(entries.shape)]
        where[longest] = (where[longest] + shift) % entries.shape[longest]
        spots.append(tuple(where))
    return entries.at[spots[0]].set(low).at[spots[1]].set(high)


def level_of(stream_key, extent, shards, least, top_value):
    factor_of = 1.0
    for dim, parts in shards:
        draws = jax.random.uniform(jax.random.fold_in(jax.random.fold_in(stream_key, 6), dim), (parts,), jnp.float32, least / len(shards), top_value / len(shards))
        factor_of = factor_of * jnp.repeat(jnp.exp(draws), extent[dim] // parts).reshape((-1,) + (1,) * (len(extent) - 1 - dim))
    return factor_of


def setup_inputs(seed: int = 0) -> dict:
    streams_of = jax.random.split(jax.random.key(seed), 7)
    labels = set_ends(jax.random.randint(streams_of[0], (NZ, NY, NX), 0, LABELS), jax.random.fold_in(streams_of[0], 1), 0, LABELS - 1).astype(jnp.int32)
    label_table = jnp.clip(jnp.exp(jax.random.uniform(streams_of[1], (LABELS, CHROMO + 1), jnp.float32, math.log(0.1), math.log(1.5))), 0.1, 1.5)
    spectra = jnp.clip(jnp.exp(math.log(2.0) - 2.3025851 * jax.random.uniform(streams_of[2], (WAVES, CHROMO + 2), jnp.float32) ** level_of(streams_of[2], (WAVES, CHROMO + 2), ((0, 2),), -0.2, 0.2)), 0.2, 2.0)
    illumination = set_ends((jax.random.randint(streams_of[3], (NY, NX), 0, 2) < 1).astype(jnp.int32), jax.random.fold_in(streams_of[3], 1), 0, 1)
    fluence_start = draw_fluence_start(jax.random.fold_in(streams_of[6], 71), 0)
    measured = jnp.clip(2.0 * jax.random.uniform(streams_of[5], (WAVES, NZ, NY, NX), jnp.float32) ** level_of(streams_of[5], (WAVES, NZ, NY, NX), ((0, 2), (1, 16)), -0.2, 0.2), 0.0, 2.0)
    return dict(labels=labels, label_table=label_table, spectra=spectra, illumination=illumination, fluence_start=fluence_start, measured=measured)


eta_step = 0.3

def neighbours(padded):
    center = padded[:, 1:-1]
    ypadded = jnp.pad(center, ((0, 0), (0, 0), (1, 1), (0, 0)))
    xpadded = jnp.pad(center, ((0, 0), (0, 0), (0, 0), (1, 1)))
    return [padded[:, 2:], padded[:, :-2], ypadded[:, :, 2:], ypadded[:, :, :-2], xpadded[:, :, :, 2:], xpadded[:, :, :, :-2]]

def optics(spectra, coeffs):
    absorb = spectra[:, 0, None, None, None] * coeffs[0][None]
    for chrom in range(1, 4):
        absorb = absorb + spectra[:, chrom, None, None, None] * coeffs[chrom][None]
    diffuse = 1.0 / (3.0 * (absorb + spectra[:, 4, None, None, None] * coeffs[4][None]))
    return (absorb, diffuse)

def face_weights(diffuse_pad):
    center = diffuse_pad[:, 1:-1]
    return [0.5 * (center + other) for other in neighbours(diffuse_pad)]

def sweep(padded, weights, total, rhs):
    accum = rhs
    for weight, other in zip(weights, neighbours(padded)):
        accum = accum + weight * other
    return accum / total

def zpad(field):
    return jnp.pad(field, ((0, 0), (1, 1), (0, 0), (0, 0)))

def reference(labels, label_table, spectra, illumination, fluence_start, measured):
    coeffs = jnp.moveaxis(label_table[labels], -1, 0)
    absorb, diffuse = optics(spectra, coeffs)
    weights = face_weights(zpad(diffuse))
    total = absorb
    for weight in weights:
        total = total + weight
    source = spectra[:, 5, None, None, None] * illumination.astype(jnp.float32)[None, None]
    fluence = fluence_start
    for step in range(ITERS):
        fluence = sweep(zpad(fluence), weights, total, source)
    misfit = absorb * fluence - measured
    adjoint = jnp.zeros_like(fluence)
    for step in range(ITERS):
        adjoint = sweep(zpad(adjoint), weights, total, absorb * misfit)
    common = fluence * (misfit - adjoint)
    grads = [lax.optimization_barrier(jnp.sum(spectra[:, chrom, None, None, None] * common, axis=0)) for chrom in range(4)]
    flu_nb = neighbours(zpad(fluence))
    adj_nb = neighbours(zpad(adjoint))
    coupling = jnp.zeros_like(fluence)
    for weight, fother, aother in zip(weights, flu_nb, adj_nb):
        coupling = coupling + weight * (fother - fluence) * (aother - adjoint)
    grads.append(lax.optimization_barrier(jnp.sum(spectra[:, 4, None, None, None] * 3.0 * diffuse * diffuse * coupling, axis=0)))
    grad = jnp.stack(grads)
    rms = jnp.sqrt(lax.optimization_barrier(jnp.sum(grad * grad, axis=(1, 2, 3))) / CELLS + 1e-06)
    updated = coeffs * jnp.exp(-eta_step * grad / rms[:, None, None, None])
    return (fluence, updated[:4], updated[4])
```

```python
import functools

import jax
import jax.numpy as jnp
from jax import lax
from jax.experimental import pallas as pl
from jax.experimental.pallas import tpu as pltpu
from jax.sharding import PartitionSpec as P

ETA = 0.3
ROWS = 32
PAD = 8
SMEM = pltpu.SMEM


def zero_rims(*pads):
    ny = pads[0].shape[1] - 2 * PAD

    @pl.when(pl.program_id(0) == 0)
    def _():
        for pad in pads:
            rim = jnp.zeros((pad.shape[0], PAD, pad.shape[2]), jnp.float32)
            pad[:, 0:PAD, :] = rim
            pad[:, PAD + ny : 2 * PAD + ny, :] = rim


def edges(n, nx):
    lane = lax.broadcasted_iota(jnp.int32, (n, nx), 1)
    return lane < nx - 1, lane > 0


def six(pad, z, r, n, masks):
    nx = pad.shape[2]
    lo = PAD + r
    c = pad[z, lo : lo + n, :]
    xp = jnp.where(masks[0], pltpu.roll(c, nx - 1, 1), 0.0)
    xm = jnp.where(masks[1], pltpu.roll(c, 1, 1), 0.0)
    return c, (
        pad[z + 1, lo : lo + n, :],
        pad[z - 1, lo : lo + n, :],
        pad[z, lo + 1 : lo + n + 1, :],
        pad[z, lo - 1 : lo + n - 1, :],
        xp,
        xm,
    )


def around(pad, z, r, n, masks):
    c, nb = six(pad, z, r, n, masks)
    return c, ((nb[0] + nb[1]) + (nb[2] + nb[3])) + (nb[4] + nb[5])


def absorption(spec, w, coef, z, rows):
    total = spec[w, 0] * coef[0, z, rows, :]
    for chrom in range(1, 4):
        total = total + spec[w, chrom] * coef[chrom, z, rows, :]
    return total


def fill(v_ref, lo_ref, hi_ref, h_ref, vpad, upad):
    nz, ny = v_ref.shape[1], v_ref.shape[2]
    mid = slice(PAD, PAD + ny)

    def put(z, v):
        vpad[z, mid, :] = v
        upad[z, mid, :] = v * h_ref[0, z]

    put(0, lo_ref[0, 0])
    put(nz + 1, hi_ref[0, 0])

    @pl.loop(0, nz)
    def _(z):
        put(z + 1, v_ref[0, z])


def ends(nz, z, r, n, value, lo_out, hi_out):
    @pl.when(z == 0)
    def _():
        lo_out[0, 0, r : r + n, :] = value

    @pl.when(z == nz - 1)
    def _():
        hi_out[0, 0, r : r + n, :] = value


def first_kernel(
    base, spec, flags, coef, illum, f_ref, flo, fhi,
    h_out, t_out, f1_out, lo_out, hi_out, hpad, vpad, upad,
):
    nz, ny, nx = f_ref.shape[1:]
    w = pl.program_id(0) + base
    zero_rims(hpad, vpad, upad)
    mid = slice(PAD, PAD + ny)

    def half(z, flag, v):
        for r in range(0, ny, ROWS):
            rows = slice(r, r + ROWS)
            here = slice(PAD + r, PAD + r + ROWS)
            absorb = absorption(spec, w, coef, z, rows)
            h = 1.0 / (6.0 * (absorb + spec[w, 4] * coef[4, z, rows, :]))
            if flag is not None:
                h = h * flag
            h_out[0, z, rows, :] = h
            hpad[z, here, :] = h
            vpad[z, here, :] = v(rows)
            upad[z, here, :] = v(rows) * h

    half(0, flags[0], lambda rows: flo[0, 0, rows, :])
    half(nz + 1, flags[1], lambda rows: fhi[0, 0, rows, :])

    @pl.loop(0, nz)
    def _(z):
        half(z + 1, None, lambda rows: f_ref[0, z, rows, :])

    masks = edges(ROWS, nx)

    @pl.loop(0, nz)
    def _(z):
        for r in range(0, ny, ROWS):
            rows = slice(r, r + ROWS)
            absorb = absorption(spec, w, coef, z + 1, rows)
            h, sh = around(hpad, z + 1, r, ROWS, masks)
            t = 1.0 / (absorb + 6.0 * h + sh)
            _, sv = around(vpad, z + 1, r, ROWS, masks)
            _, su = around(upad, z + 1, r, ROWS, masks)
            source = spec[w, 5] * illum[rows, :].astype(jnp.float32)
            f1 = (source + h * sv + su) * t
            t_out[0, z, rows, :] = t
            f1_out[0, z, rows, :] = f1
            ends(nz, z, r, ROWS, f1, lo_out, hi_out)


def second_kernel(
    base, spec, coef, illum, v_ref, lo_ref, hi_ref, h_ref, t_ref, m_ref, *rest
):
    f2_out, a1_out, flo_out, fhi_out, alo_out, ahi_out, vpad, upad = rest[-8:]
    nz, ny, nx = v_ref.shape[1:]
    w = pl.program_id(0) + base
    zero_rims(vpad, upad)
    fill(v_ref, lo_ref, hi_ref, h_ref, vpad, upad)
    masks = edges(ROWS, nx)

    @pl.loop(0, nz)
    def _(z):
        for r in range(0, ny, ROWS):
            rows = slice(r, r + ROWS)
            absorb = absorption(spec, w, coef, z + 1, rows)
            _, sv = around(vpad, z + 1, r, ROWS, masks)
            _, su = around(upad, z + 1, r, ROWS, masks)
            t = t_ref[0, z, rows, :]
            source = spec[w, 5] * illum[rows, :].astype(jnp.float32)
            f2 = (source + h_ref[0, z + 1, rows, :] * sv + su) * t
            a1 = absorb * (absorb * f2 - m_ref[0, z, rows, :]) * t
            f2_out[0, z, rows, :] = f2
            a1_out[0, z, rows, :] = a1
            ends(nz, z, r, ROWS, f2, flo_out, fhi_out)
            ends(nz, z, r, ROWS, a1, alo_out, ahi_out)


def third_kernel(
    base, spec, coef, v_ref, lo_ref, hi_ref, h_ref, t_ref, m_ref, f2_ref, *rest
):
    a2_out, alo_out, ahi_out, g_out, vpad, upad = rest[-6:]
    prior = rest[0] if len(rest) == 7 else None
    nz, ny, nx = v_ref.shape[1:]
    w = pl.program_id(0) + base
    zero_rims(vpad, upad)
    fill(v_ref, lo_ref, hi_ref, h_ref, vpad, upad)
    masks = edges(ROWS, nx)

    @pl.when(pl.program_id(0) == 0)
    def _():
        if prior is None:
            g_out[...] = jnp.zeros_like(g_out)
        else:
            g_out[...] = prior[...]

    @pl.loop(0, nz)
    def _(z):
        for r in range(0, ny, ROWS):
            rows = slice(r, r + ROWS)
            absorb = absorption(spec, w, coef, z + 1, rows)
            a1, sv = around(vpad, z + 1, r, ROWS, masks)
            _, su = around(upad, z + 1, r, ROWS, masks)
            a2 = a1 + (h_ref[0, z + 1, rows, :] * sv + su) * t_ref[0, z, rows, :]
            a2_out[0, z, rows, :] = a2
            ends(nz, z, r, ROWS, a2, alo_out, ahi_out)
            f2 = f2_ref[0, z, rows, :]
            common = f2 * ((absorb * f2 - m_ref[0, z, rows, :]) - a2)
            for chrom in range(4):
                g_out[chrom, z, rows, :] += spec[w, chrom] * common


def fourth_kernel(
    base, spec, f_ref, flo, fhi, a_ref, alo, ahi, h_ref, *rest
):
    g_out, fpad, apad, hpad = rest[-4:]
    prior = rest[0] if len(rest) == 5 else None
    nz, ny, nx = f_ref.shape[1:]
    w = pl.program_id(0) + base
    zero_rims(fpad, apad, hpad)
    mid = slice(PAD, PAD + ny)
    fpad[0, mid, :] = flo[0, 0]
    apad[0, mid, :] = alo[0, 0]
    hpad[0, mid, :] = h_ref[0, 0]
    fpad[nz + 1, mid, :] = fhi[0, 0]
    apad[nz + 1, mid, :] = ahi[0, 0]
    hpad[nz + 1, mid, :] = h_ref[0, nz + 1]

    @pl.loop(0, nz)
    def _(z):
        fpad[z + 1, mid, :] = f_ref[0, z]
        apad[z + 1, mid, :] = a_ref[0, z]
        hpad[z + 1, mid, :] = h_ref[0, z + 1]

    @pl.when(pl.program_id(0) == 0)
    def _():
        if prior is None:
            g_out[...] = jnp.zeros_like(g_out)
        else:
            g_out[...] = prior[...]

    masks = edges(ROWS, nx)

    @pl.loop(0, nz)
    def _(z):
        for r in range(0, ny, ROWS):
            rows = slice(r, r + ROWS)
            f, fn = six(fpad, z + 1, r, ROWS, masks)
            a, an = six(apad, z + 1, r, ROWS, masks)
            h, hn = six(hpad, z + 1, r, ROWS, masks)
            coupling = jnp.zeros_like(f)
            for hs, fs, ls in zip(hn, fn, an):
                coupling = coupling + (h + hs) * ((fs - f) * (ls - a))
            g_out[z, rows, :] += (12.0 * spec[w, 4]) * (h * h) * coupling


def sweeps(spectra, flags, coef, illum, start, measured, exchange, groups):
    waves, nz, ny, nx = start.shape
    per = waves // groups
    f32 = jnp.float32

    def own(*shape):
        return jax.ShapeDtypeStruct(shape, f32)

    def blk(planes, base=0):
        return pl.BlockSpec((1, planes, ny, nx), lambda i: (i + base, 0, 0, 0))

    def fixed(*shape):
        return pl.BlockSpec(shape, lambda i: (0,) * len(shape))

    smem = pl.BlockSpec(memory_space=SMEM)
    anyspace = pl.BlockSpec(memory_space=pl.ANY)
    coefs, light = fixed(*coef.shape), fixed(ny, nx)
    field, plane, thick = own(per, nz, ny, nx), own(per, 1, ny, nx), own(per, nz + 2, ny, nx)
    pad = pltpu.VMEM((nz + 2, ny + 2 * PAD, nx), f32)

    def call(kernel, base, in_specs, out_shape, out_specs, scratch, ops, alias, *operands):
        cells = per * nz * ny * nx
        return pl.pallas_call(
            functools.partial(kernel, base),
            grid=(per,),
            in_specs=in_specs,
            out_shape=out_shape,
            out_specs=out_specs,
            scratch_shapes=scratch,
            input_output_aliases=alias,
            cost_estimate=pl.CostEstimate(
                flops=cells * ops, bytes_accessed=cells * 24, transcendentals=0
            ),
            compiler_params=pltpu.CompilerParams(vmem_limit_bytes=40 * 1024 * 1024),
        )(*operands)

    bases = [g * per for g in range(groups)]
    started = [
        exchange(start[b : b + per, :1], start[b : b + per, nz - 1 :]) for b in bases
    ]
    halves, inverses, firsts, firsts_nb = [], [], [], []
    for g, b in enumerate(bases):
        h, t, f1, lo, hi = call(
            first_kernel, b,
            [smem, smem, coefs, light, blk(nz, b), blk(1), blk(1)],
            [thick, field, field, plane, plane],
            [blk(nz + 2), blk(nz), blk(nz), blk(1), blk(1)],
            [pad, pad, pad], 60, {},
            spectra, flags, coef, illum, start, *started[g],
        )
        halves.append(h)
        inverses.append(t)
        firsts.append(f1)
        firsts_nb.append(exchange(lo, hi))

    fluence, a1s, a1_nb, f2_nb = None, [], [], []
    for g, b in enumerate(bases):
        more = [] if fluence is None else [fluence]
        fluence, a1, flo, fhi, alo, ahi = call(
            second_kernel, b,
            [smem, coefs, light, blk(nz), blk(1), blk(1), blk(nz + 2), blk(nz), blk(nz, b)]
            + [anyspace] * len(more),
            [own(waves, nz, ny, nx), field, plane, plane, plane, plane],
            [blk(nz, b), blk(nz), blk(1), blk(1), blk(1), blk(1)],
            [pad, pad], 40, {9: 0} if more else {},
            spectra, coef, illum, firsts[g], *firsts_nb[g], halves[g], inverses[g], measured,
            *more,
        )
        a1s.append(a1)
        a1_nb.append(exchange(alo, ahi))
        f2_nb.append(exchange(flo, fhi))

    chrom, a2s, a2_nb = None, [], []
    for g, b in enumerate(bases):
        more = [] if chrom is None else [chrom]
        a2, alo, ahi, chrom = call(
            third_kernel, b,
            [smem, coefs, blk(nz), blk(1), blk(1), blk(nz + 2), blk(nz), blk(nz, b), blk(nz, b)]
            + [fixed(4, nz, ny, nx)] * len(more),
            [field, plane, plane, own(4, nz, ny, nx)],
            [blk(nz), blk(1), blk(1), fixed(4, nz, ny, nx)],
            [pad, pad], 50, {},
            spectra, coef, a1s[g], *a1_nb[g], halves[g], inverses[g], measured, fluence, *more,
        )
        a2s.append(a2)
        a2_nb.append(exchange(alo, ahi))

    scatter = None
    for g, b in enumerate(bases):
        more = [] if scatter is None else [scatter]
        scatter = call(
            fourth_kernel, b,
            [smem, blk(nz, b), blk(1), blk(1), blk(nz), blk(1), blk(1), blk(nz + 2)]
            + [fixed(nz, ny, nx)] * len(more),
            own(nz, ny, nx),
            fixed(nz, ny, nx),
            [pad, pad, pad], 60, {},
            spectra, fluence, *f2_nb[g], a2s[g], *a2_nb[g], halves[g], *more,
        )
    return fluence, chrom, scatter


def shards(labels, label_table, spectra, illumination, fluence_start, measured):
    count = lax.axis_size("gz")
    index = lax.axis_index("gz")
    forward = [(i, i + 1) for i in range(count - 1)]
    backward = [(target, source) for source, target in forward]

    def exchange(low_plane, high_plane):
        return (
            lax.ppermute(high_plane, "gz", forward),
            lax.ppermute(low_plane, "gz", backward),
        )

    wl = lax.axis_size("wl")

    def wl_sum(part):
        if wl == 2:
            return part + lax.ppermute(part, "wl", [(0, 1), (1, 0)])
        return lax.psum(part, "wl")

    nz, ny, nx = labels.shape
    below, above = exchange(labels[:1], labels[nz - 1 :])
    classes = jnp.concatenate([below, labels, above], axis=0)

    def lookup(column):
        value = jnp.broadcast_to(label_table[0, column], classes.shape)
        for k in range(1, label_table.shape[0]):
            value = jnp.where(classes == k, label_table[k, column], value)
        return value

    coef = jnp.stack([lookup(column) for column in range(5)])
    flags = jnp.stack([index > 0, index < count - 1]).astype(jnp.float32)
    groups = 2 if spectra.shape[0] % 2 == 0 else 1
    fluence, chrom, scatter = sweeps(
        spectra, flags, coef, illumination, fluence_start, measured, exchange, groups
    )
    chrom_sum = wl_sum(chrom)
    scatter_sum = wl_sum(scatter)
    squares = jnp.concatenate(
        [jnp.sum(chrom_sum * chrom_sum, axis=(1, 2, 3)), jnp.sum(scatter_sum * scatter_sum)[None]]
    )
    cells = nz * count * ny * nx
    rms = jnp.sqrt(lax.psum(squares, "gz") / cells + 1e-06)
    center = coef[:, 1 : nz + 1]
    concentrations = center[:4] * jnp.exp(-ETA * chrom_sum / rms[:4, None, None, None])
    scattering = center[4] * jnp.exp(-ETA * scatter_sum / rms[4])
    return fluence, concentrations, scattering


def solution(mesh):
    in_specs = (
        P("gz", None, None),
        P(),
        P("wl", None),
        P(),
        P("wl", "gz", None, None),
        P("wl", "gz", None, None),
    )
    out_specs = (P("wl", "gz", None, None), P(None, "gz", None, None), P("gz", None, None))
    return jax.shard_map(shards, mesh=mesh, in_specs=in_specs, out_specs=out_specs, check_vma=False)
```

```python
import functools

import jax
import jax.numpy as jnp
from jax import lax
from jax.experimental import pallas as pl
from jax.experimental.pallas import tpu as pltpu
from jax.sharding import PartitionSpec as P

ETA = 0.3
ROWS = 32
PAD = 8
SMEM = pltpu.SMEM
MESH = pl.DeviceIdType.MESH
START, ONCE, FLUENCE, FIRST, ADJOINT = range(5)


def edges(n, nx):
    lane = lax.broadcasted_iota(jnp.int32, (n, nx), 1)
    return lane < nx - 1, lane > 0


def six(pad, z, r, n, masks):
    nx = pad.shape[2]
    lo = PAD + r
    c = pad[z, lo : lo + n, :]
    xp = jnp.where(masks[0], pltpu.roll(c, nx - 1, 1), 0.0)
    xm = jnp.where(masks[1], pltpu.roll(c, 1, 1), 0.0)
    return c, (
        pad[z + 1, lo : lo + n, :],
        pad[z - 1, lo : lo + n, :],
        pad[z, lo + 1 : lo + n + 1, :],
        pad[z, lo - 1 : lo + n - 1, :],
        xp,
        xm,
    )


def around(pad, z, r, n, masks):
    c, nb = six(pad, z, r, n, masks)
    return c, ((nb[0] + nb[1]) + (nb[2] + nb[3])) + (nb[4] + nb[5])


def absorption(spec, w, coef, z, rows):
    total = spec[w, 0] * coef[0, z, rows, :]
    for chrom in range(1, 4):
        total = total + spec[w, chrom] * coef[chrom, z, rows, :]
    return total


def kernel(
    per, spec, table, labels, illum, start, measured,
    f_out, grad, coef,
    field, other, half, inverse, meas, halos, tags, vpad, upad, wpad, partner,
    send_sem, recv_sem, tag_send, tag_recv, in_sem, out_sem, meas_sem, g_send, g_recv,
):
    waves, nz, ny, nx = field.shape
    chunks = waves // per
    peers = lax.axis_size("wl") - 1
    count = lax.axis_size("gz")
    idx = lax.axis_index("gz")
    has_lo, has_hi = idx > 0, idx < count - 1
    above, below = lax.rem(idx + 1, count), lax.rem(idx + count - 1, count)
    mine = lax.axis_index("wl")
    mid = slice(PAD, PAD + ny)
    masks = edges(ROWS, nx)

    barrier = pltpu.get_barrier_semaphore()

    def greet(axis, where):
        pl.semaphore_signal(barrier, inc=1, device_id={axis: where}, device_id_type=MESH)

    pl.when(has_hi)(lambda: greet("gz", above))
    pl.when(has_lo)(lambda: greet("gz", below))
    for k in range(peers):
        greet("wl", lax.rem(mine + k + 1, peers + 1))

    def loaded(c):
        rows = pl.ds(c * per, per)
        return pltpu.make_async_copy(start.at[rows], field.at[rows], in_sem.at[c])

    def stored(c):
        rows = pl.ds(c * per, per)
        return pltpu.make_async_copy(field.at[rows], f_out.at[rows], out_sem.at[c])

    def measure(c):
        slot = lax.rem(c, 2)
        return pltpu.make_async_copy(
            measured.at[pl.ds(c * per, per)], meas.at[slot], meas_sem.at[slot]
        )

    @pl.loop(0, chunks)
    def _(c):
        loaded(c).start()

    def halo(kind, side, c):
        rows = pl.ds(c * per, per)
        plane = nz - 1 if side == 0 else 0
        source = {START: start, FLUENCE: field}.get(kind, other)
        return pltpu.make_async_remote_copy(
            src_ref=source.at[rows, plane],
            dst_ref=halos.at[kind, side, rows],
            send_sem=send_sem.at[kind, side, c],
            recv_sem=recv_sem.at[kind, side, c],
            device_id={"gz": above if side == 0 else below},
            device_id_type=MESH,
        )

    def tag(side):
        return pltpu.make_async_remote_copy(
            src_ref=labels.at[nz - 1 if side == 0 else 0],
            dst_ref=tags.at[side],
            send_sem=tag_send.at[side],
            recv_sem=tag_recv.at[side],
            device_id={"gz": above if side == 0 else below},
            device_id_type=MESH,
        )

    def send(make):
        pl.when(has_hi)(lambda: make(0).start())
        pl.when(has_lo)(lambda: make(1).start())

    def arrive(make):
        pl.when(has_lo)(lambda: make(0).wait_recv())
        pl.when(has_hi)(lambda: make(1).wait_recv())

    def left(make):
        pl.when(has_hi)(lambda: make(0).wait_send())
        pl.when(has_lo)(lambda: make(1).wait_send())

    def blank(side):
        tags[side] = jnp.zeros((ny, nx), jnp.int32)

        @pl.loop(0, 5)
        def _(kind):
            @pl.loop(0, waves)
            def _(w):
                halos[kind, side, w] = jnp.zeros((ny, nx), jnp.float32)

    pl.when(jnp.logical_not(has_lo))(lambda: blank(0))
    pl.when(jnp.logical_not(has_hi))(lambda: blank(1))

    pl.semaphore_wait(barrier, has_lo.astype(jnp.int32) + has_hi.astype(jnp.int32) + peers)

    send(tag)

    @pl.loop(0, chunks)
    def _(c):
        send(lambda side: halo(START, side, c))

    rim = jnp.zeros((nz + 2, PAD, nx), jnp.float32)
    for pad in (vpad, upad, wpad):
        pad[:, 0:PAD, :] = rim
        pad[:, PAD + ny : 2 * PAD + ny, :] = rim

    @pl.loop(0, nz)
    def _(z):
        grad[:, z] = jnp.zeros((5, ny, nx), jnp.float32)

    def lookup(z, classes):
        for r in range(0, ny, ROWS):
            tags_here = classes(slice(r, r + ROWS))
            same = [tags_here == k for k in range(1, table.shape[0])]
            for column in range(5):
                value = jnp.full((ROWS, nx), table[0, column], jnp.float32)
                for k, hit in enumerate(same):
                    value = jnp.where(hit, table[k + 1, column], value)
                coef[column, z, r : r + ROWS, :] = value

    @pl.loop(0, nz)
    def _(z):
        lookup(z + 1, lambda rows: labels[z, rows, :])

    arrive(tag)
    lookup(0, lambda rows: tags[0, rows, :])
    lookup(nz + 1, lambda rows: tags[1, rows, :])

    lo_flag, hi_flag = has_lo.astype(jnp.float32), has_hi.astype(jnp.float32)

    def each_wave(c, body):
        @pl.loop(0, per)
        def _(j):
            body(c * per + j, j)

    def each_tile(body):
        @pl.loop(0, nz)
        def _(z):
            for r in range(0, ny, ROWS):
                body(z, r, slice(r, r + ROWS))

    def fill(kind, w, values):
        def put(z, v):
            vpad[z, mid, :] = v
            upad[z, mid, :] = v * half[w, z]

        put(0, halos[kind, 0, w])
        put(nz + 1, halos[kind, 1, w])

        @pl.loop(0, nz)
        def _(z):
            put(z + 1, values[w, z])

    def once(w, _):
        def optics(z, flag, v):
            for r in range(0, ny, ROWS):
                rows = slice(r, r + ROWS)
                here = slice(PAD + r, PAD + r + ROWS)
                absorb = absorption(spec, w, coef, z, rows)
                h = 1.0 / (6.0 * (absorb + spec[w, 4] * coef[4, z, rows, :]))
                if flag is not None:
                    h = h * flag
                value = v(rows)
                half[w, z, rows, :] = h
                wpad[z, here, :] = h
                vpad[z, here, :] = value
                upad[z, here, :] = value * h

        optics(0, lo_flag, lambda rows: halos[START, 0, w, rows, :])
        optics(nz + 1, hi_flag, lambda rows: halos[START, 1, w, rows, :])

        @pl.loop(0, nz)
        def _(z):
            optics(z + 1, None, lambda rows: field[w, z, rows, :])

        def tile(z, r, rows):
            absorb = absorption(spec, w, coef, z + 1, rows)
            h, sh = around(wpad, z + 1, r, ROWS, masks)
            t = 1.0 / (absorb + 6.0 * h + sh)
            _, sv = around(vpad, z + 1, r, ROWS, masks)
            _, su = around(upad, z + 1, r, ROWS, masks)
            source = spec[w, 5] * illum[rows, :].astype(jnp.float32)
            inverse[w, z, rows, :] = t
            other[w, z, rows, :] = (source + h * sv + su) * t

        each_tile(tile)

    @pl.loop(0, chunks)
    def _(c):
        loaded(c).wait()
        arrive(lambda side: halo(START, side, c))
        each_wave(c, once)
        send(lambda side: halo(ONCE, side, c))

    def twice(c):
        def body(w, j):
            fill(ONCE, w, other)
            slot = lax.rem(c, 2)

            def tile(z, r, rows):
                absorb = absorption(spec, w, coef, z + 1, rows)
                _, sv = around(vpad, z + 1, r, ROWS, masks)
                _, su = around(upad, z + 1, r, ROWS, masks)
                t = inverse[w, z, rows, :]
                source = spec[w, 5] * illum[rows, :].astype(jnp.float32)
                f2 = (source + half[w, z + 1, rows, :] * sv + su) * t
                field[w, z, rows, :] = f2
                other[w, z, rows, :] = absorb * (absorb * f2 - meas[slot, j, z, rows, :]) * t

            each_tile(tile)

        return body

    def with_measured(body):
        measure(0).start()

        @pl.loop(0, chunks)
        def _(c):
            pl.when(c + 1 < chunks)(lambda: measure(c + 1).start())
            measure(c).wait()
            body(c)

    def second(c):
        arrive(lambda side: halo(ONCE, side, c))
        left(lambda side: halo(ONCE, side, c))
        left(lambda side: halo(START, side, c))
        each_wave(c, twice(c))
        send(lambda side: halo(FIRST, side, c))
        send(lambda side: halo(FLUENCE, side, c))
        stored(c).start()

    with_measured(second)

    def adjoint(c):
        def body(w, j):
            fill(FIRST, w, other)
            slot = lax.rem(c, 2)

            def tile(z, r, rows):
                absorb = absorption(spec, w, coef, z + 1, rows)
                a1, sv = around(vpad, z + 1, r, ROWS, masks)
                _, su = around(upad, z + 1, r, ROWS, masks)
                a2 = a1 + (half[w, z + 1, rows, :] * sv + su) * inverse[w, z, rows, :]
                other[w, z, rows, :] = a2
                f2 = field[w, z, rows, :]
                common = f2 * ((absorb * f2 - meas[slot, j, z, rows, :]) - a2)
                for chrom in range(4):
                    grad[chrom, z, rows, :] += spec[w, chrom] * common

            each_tile(tile)

        return body

    def third(c):
        arrive(lambda side: halo(FIRST, side, c))
        left(lambda side: halo(FIRST, side, c))
        each_wave(c, adjoint(c))
        send(lambda side: halo(ADJOINT, side, c))

    with_measured(third)

    def share(k, lo, n, part):
        return pltpu.make_async_remote_copy(
            src_ref=grad.at[pl.ds(lo, n)],
            dst_ref=partner.at[k, pl.ds(lo, n)],
            send_sem=g_send.at[k, part],
            recv_sem=g_recv.at[k, part],
            device_id={"wl": lax.rem(mine + k + 1, peers + 1)},
            device_id_type=MESH,
        )

    for k in range(peers):
        share(k, 0, 4, 0).start()

    def scatter(w, _):
        fpad, apad = vpad, upad
        for z, side in ((0, 0), (nz + 1, 1)):
            fpad[z, mid, :] = halos[FLUENCE, side, w]
            apad[z, mid, :] = halos[ADJOINT, side, w]
            wpad[z, mid, :] = half[w, z]

        @pl.loop(0, nz)
        def _(z):
            fpad[z + 1, mid, :] = field[w, z]
            apad[z + 1, mid, :] = other[w, z]
            wpad[z + 1, mid, :] = half[w, z + 1]

        def tile(z, r, rows):
            f, fn = six(fpad, z + 1, r, ROWS, masks)
            a, an = six(apad, z + 1, r, ROWS, masks)
            h, hn = six(wpad, z + 1, r, ROWS, masks)
            coupling = jnp.zeros_like(f)
            for hs, fs, ls in zip(hn, fn, an):
                coupling = coupling + (h + hs) * ((fs - f) * (ls - a))
            grad[4, z, rows, :] += (12.0 * spec[w, 4]) * (h * h) * coupling

        each_tile(tile)

    @pl.loop(0, chunks)
    def _(c):
        arrive(lambda side: halo(FLUENCE, side, c))
        arrive(lambda side: halo(ADJOINT, side, c))
        each_wave(c, scatter)

    for k in range(peers):
        share(k, 4, 1, 1).start()

    @pl.loop(0, chunks)
    def _(c):
        left(lambda side: halo(FLUENCE, side, c))
        left(lambda side: halo(ADJOINT, side, c))
        stored(c).wait()

    left(tag)
    for k in range(peers):
        share(k, 0, 4, 0).wait()
        share(k, 4, 1, 1).wait()

    @pl.loop(0, nz)
    def _(z):
        for column in range(5):
            total = grad[column, z]
            for k in range(peers):
                total = total + partner[k, column, z]
            grad[column, z] = total


def shards(labels, label_table, spectra, illumination, fluence_start, measured):
    waves, nz, ny, nx = fluence_start.shape
    per = 2 if waves % 2 == 0 else 1
    chunks = waves // per
    peers = lax.axis_size("wl") - 1
    slots = max(peers, 1)
    f32 = jnp.float32
    dma = pltpu.SemaphoreType.DMA
    smem = pl.BlockSpec(memory_space=SMEM)
    vmem = pl.BlockSpec(memory_space=pltpu.VMEM)
    anyspace = pl.BlockSpec(memory_space=pl.ANY)
    whole = pltpu.VMEM((waves, nz, ny, nx), f32)
    pad = pltpu.VMEM((nz + 2, ny + 2 * PAD, nx), f32)
    fluence, grad, coef = pl.pallas_call(
        functools.partial(kernel, per),
        in_specs=[smem, smem, vmem, vmem, anyspace, anyspace],
        out_specs=[anyspace, vmem, vmem],
        out_shape=[
            jax.ShapeDtypeStruct((waves, nz, ny, nx), f32),
            jax.ShapeDtypeStruct((5, nz, ny, nx), f32),
            jax.ShapeDtypeStruct((5, nz + 2, ny, nx), f32),
        ],
        scratch_shapes=[
            whole,
            whole,
            pltpu.VMEM((waves, nz + 2, ny, nx), f32),
            whole,
            pltpu.VMEM((2, per, nz, ny, nx), f32),
            pltpu.VMEM((5, 2, waves, ny, nx), f32),
            pltpu.VMEM((2, ny, nx), jnp.int32),
            pad,
            pad,
            pad,
            pltpu.VMEM((slots, 5, nz, ny, nx), f32),
            dma((5, 2, chunks)),
            dma((5, 2, chunks)),
            dma((2,)),
            dma((2,)),
            dma((chunks,)),
            dma((chunks,)),
            dma((2,)),
            dma((slots, 2)),
            dma((slots, 2)),
        ],
        cost_estimate=pl.CostEstimate(
            flops=waves * nz * ny * nx * 200,
            bytes_accessed=waves * nz * ny * nx * 16,
            transcendentals=0,
        ),
        compiler_params=pltpu.CompilerParams(
            collective_id=0, has_side_effects=True, vmem_limit_bytes=62 * 1024 * 1024
        ),
    )(spectra, label_table, labels, illumination, fluence_start, measured)
    squares = jnp.sum(grad * grad, axis=(1, 2, 3))
    cells = nz * lax.axis_size("gz") * ny * nx
    rms = jnp.sqrt(lax.psum(squares, "gz") / cells + 1e-06)
    updated = coef[:, 1 : nz + 1] * jnp.exp(-ETA * grad / rms[:, None, None, None])
    return fluence, updated[:4], updated[4]


def solution(mesh):
    in_specs = (
        P("gz", None, None),
        P(),
        P("wl", None),
        P(),
        P("wl", "gz", None, None),
        P("wl", "gz", None, None),
    )
    out_specs = (P("wl", "gz", None, None), P(None, "gz", None, None), P("gz", None, None))
    return jax.shard_map(shards, mesh=mesh, in_specs=in_specs, out_specs=out_specs, check_vma=False)
```

```python
import functools

import jax
import jax.numpy as jnp
from jax import lax
from jax.experimental import pallas as pl
from jax.experimental.pallas import tpu as pltpu
from jax.sharding import PartitionSpec as P

ETA = 0.3
ROWS = 64
PAD = 8
SMEM = pltpu.SMEM
MESH = pl.DeviceIdType.MESH
START, ONCE, FLUENCE, FIRST, ADJOINT = range(5)


def edges(n, nx):
    lane = lax.broadcasted_iota(jnp.int32, (n, nx), 1)
    return lane < nx - 1, lane > 0


def six(pad, z, r, n, masks):
    nx = pad.shape[2]
    lo = PAD + r
    c = pad[z, lo : lo + n, :]
    xp = jnp.where(masks[0], pltpu.roll(c, nx - 1, 1), 0.0)
    xm = jnp.where(masks[1], pltpu.roll(c, 1, 1), 0.0)
    return c, (
        pad[z + 1, lo : lo + n, :],
        pad[z - 1, lo : lo + n, :],
        pad[z, lo + 1 : lo + n + 1, :],
        pad[z, lo - 1 : lo + n - 1, :],
        xp,
        xm,
    )


def around(pad, z, r, n, masks):
    c, nb = six(pad, z, r, n, masks)
    return c, ((nb[0] + nb[1]) + (nb[2] + nb[3])) + (nb[4] + nb[5])


def absorption(spec, w, coef, z, rows):
    total = spec[w, 0] * coef[0, z, rows, :]
    for chrom in range(1, 4):
        total = total + spec[w, chrom] * coef[chrom, z, rows, :]
    return total


def rounds_of(count):
    stride, rounds = 1, []
    while stride < count:
        rest = count // stride
        radix = 4 if rest % 4 == 0 else 2 if rest % 2 == 0 else rest
        rounds.append((stride, radix))
        stride *= radix
    return rounds


def kernel(
    per, spec, table, labels, illum, start, measured,
    f_out, chroms, scats,
    coef, field, other, half, inverse, meas, halos, tags, vpad, upad, wpad, partner, sums, sums_in,
    send_sem, recv_sem, tag_send, tag_recv, in_sem, out_sem, meas_sem, g_send, g_recv, s_send, s_recv,
):
    waves, nz, ny, nx = field.shape
    chunks = waves // per
    peers = lax.axis_size("wl") - 1
    count = lax.axis_size("gz")
    idx = lax.axis_index("gz")
    has_lo, has_hi = idx > 0, idx < count - 1
    above, below = lax.rem(idx + 1, count), lax.rem(idx + count - 1, count)
    mine = lax.axis_index("wl")
    mid = slice(PAD, PAD + ny)
    masks = edges(ROWS, nx)

    barrier = pltpu.get_barrier_semaphore()

    def greet(axis, where):
        pl.semaphore_signal(barrier, inc=1, device_id={axis: where}, device_id_type=MESH)

    pl.when(has_hi)(lambda: greet("gz", above))
    pl.when(has_lo)(lambda: greet("gz", below))
    for k in range(peers):
        greet("wl", lax.rem(mine + k + 1, peers + 1))

    rounds = rounds_of(count)

    def fellow(step, k):
        stride, radix = rounds[step]
        digit = lax.rem(lax.div(idx, stride), radix)
        return idx + (lax.rem(digit + k, radix) - digit) * stride

    for step, (_, radix) in enumerate(rounds):
        for k in range(1, radix):
            greet("gz", fellow(step, k))
    met = peers + sum(radix - 1 for _, radix in rounds)

    def loaded(c):
        rows = pl.ds(c * per, per)
        return pltpu.make_async_copy(start.at[rows], field.at[rows], in_sem.at[c])

    def stored(c):
        rows = pl.ds(c * per, per)
        return pltpu.make_async_copy(field.at[rows], f_out.at[rows], out_sem.at[c])

    def measure(c):
        slot = lax.rem(c, 2)
        return pltpu.make_async_copy(
            measured.at[pl.ds(c * per, per)], meas.at[slot], meas_sem.at[slot]
        )

    @pl.loop(0, chunks)
    def _(c):
        loaded(c).start()

    def halo(kind, side, c):
        rows = pl.ds(c * per, per)
        plane = nz - 1 if side == 0 else 0
        source = {START: start, FLUENCE: field}.get(kind, other)
        return pltpu.make_async_remote_copy(
            src_ref=source.at[rows, plane],
            dst_ref=halos.at[kind, side, rows],
            send_sem=send_sem.at[kind, side, c],
            recv_sem=recv_sem.at[kind, side, c],
            device_id={"gz": above if side == 0 else below},
            device_id_type=MESH,
        )

    def tag(side):
        return pltpu.make_async_remote_copy(
            src_ref=labels.at[nz - 1 if side == 0 else 0],
            dst_ref=tags.at[side],
            send_sem=tag_send.at[side],
            recv_sem=tag_recv.at[side],
            device_id={"gz": above if side == 0 else below},
            device_id_type=MESH,
        )

    def send(make):
        pl.when(has_hi)(lambda: make(0).start())
        pl.when(has_lo)(lambda: make(1).start())

    def arrive(make):
        pl.when(has_lo)(lambda: make(0).wait_recv())
        pl.when(has_hi)(lambda: make(1).wait_recv())

    def left(make):
        pl.when(has_hi)(lambda: make(0).wait_send())
        pl.when(has_lo)(lambda: make(1).wait_send())

    def blank(side):
        tags[side] = jnp.zeros((ny, nx), jnp.int32)

        @pl.loop(0, 5)
        def _(kind):
            @pl.loop(0, waves)
            def _(w):
                halos[kind, side, w] = jnp.zeros((ny, nx), jnp.float32)

    pl.when(jnp.logical_not(has_lo))(lambda: blank(0))
    pl.when(jnp.logical_not(has_hi))(lambda: blank(1))

    pl.semaphore_wait(barrier, has_lo.astype(jnp.int32) + has_hi.astype(jnp.int32) + met)

    send(tag)

    @pl.loop(0, chunks)
    def _(c):
        send(lambda side: halo(START, side, c))

    rim = jnp.zeros((nz + 2, PAD, nx), jnp.float32)
    for pad in (vpad, upad, wpad):
        pad[:, 0:PAD, :] = rim
        pad[:, PAD + ny : 2 * PAD + ny, :] = rim

    @pl.loop(0, nz)
    def _(z):
        chroms[:, z] = jnp.zeros((4, ny, nx), jnp.float32)
        scats[z] = jnp.zeros((ny, nx), jnp.float32)

    def lookup(z, classes):
        for r in range(0, ny, ROWS):
            tags_here = classes(slice(r, r + ROWS))
            same = [tags_here == k for k in range(1, table.shape[0])]
            for column in range(5):
                value = jnp.full((ROWS, nx), table[0, column], jnp.float32)
                for k, hit in enumerate(same):
                    value = jnp.where(hit, table[k + 1, column], value)
                coef[column, z, r : r + ROWS, :] = value

    @pl.loop(0, nz)
    def _(z):
        lookup(z + 1, lambda rows: labels[z, rows, :])

    arrive(tag)
    lookup(0, lambda rows: tags[0, rows, :])
    lookup(nz + 1, lambda rows: tags[1, rows, :])

    lo_flag, hi_flag = has_lo.astype(jnp.float32), has_hi.astype(jnp.float32)

    def each_wave(c, body):
        @pl.loop(0, per)
        def _(j):
            body(c * per + j, j)

    def each_tile(body):
        @pl.loop(0, nz)
        def _(z):
            for r in range(0, ny, ROWS):
                body(z, r, slice(r, r + ROWS))

    def fill(kind, w, values):
        def put(z, v):
            vpad[z, mid, :] = v
            upad[z, mid, :] = v * half[w, z]

        put(0, halos[kind, 0, w])
        put(nz + 1, halos[kind, 1, w])

        @pl.loop(0, nz)
        def _(z):
            put(z + 1, values[w, z])

    def once(w, _):
        def optics(z, flag, v):
            for r in range(0, ny, ROWS):
                rows = slice(r, r + ROWS)
                here = slice(PAD + r, PAD + r + ROWS)
                absorb = absorption(spec, w, coef, z, rows)
                h = 1.0 / (6.0 * (absorb + spec[w, 4] * coef[4, z, rows, :]))
                if flag is not None:
                    h = h * flag
                value = v(rows)
                half[w, z, rows, :] = h
                wpad[z, here, :] = h
                vpad[z, here, :] = value
                upad[z, here, :] = value * h

        optics(0, lo_flag, lambda rows: halos[START, 0, w, rows, :])
        optics(nz + 1, hi_flag, lambda rows: halos[START, 1, w, rows, :])

        @pl.loop(0, nz)
        def _(z):
            optics(z + 1, None, lambda rows: field[w, z, rows, :])

        def tile(z, r, rows):
            absorb = absorption(spec, w, coef, z + 1, rows)
            h, sh = around(wpad, z + 1, r, ROWS, masks)
            t = 1.0 / (absorb + 6.0 * h + sh)
            _, sv = around(vpad, z + 1, r, ROWS, masks)
            _, su = around(upad, z + 1, r, ROWS, masks)
            source = spec[w, 5] * illum[rows, :].astype(jnp.float32)
            inverse[w, z, rows, :] = t
            other[w, z, rows, :] = (source + h * sv + su) * t

        each_tile(tile)

    @pl.loop(0, chunks)
    def _(c):
        loaded(c).wait()
        arrive(lambda side: halo(START, side, c))
        each_wave(c, once)
        send(lambda side: halo(ONCE, side, c))

    def twice(c):
        def body(w, j):
            fill(ONCE, w, other)
            slot = lax.rem(c, 2)

            def tile(z, r, rows):
                absorb = absorption(spec, w, coef, z + 1, rows)
                _, sv = around(vpad, z + 1, r, ROWS, masks)
                _, su = around(upad, z + 1, r, ROWS, masks)
                t = inverse[w, z, rows, :]
                source = spec[w, 5] * illum[rows, :].astype(jnp.float32)
                f2 = (source + half[w, z + 1, rows, :] * sv + su) * t
                field[w, z, rows, :] = f2
                other[w, z, rows, :] = absorb * (absorb * f2 - meas[slot, j, z, rows, :]) * t

            each_tile(tile)

        return body

    def with_measured(body):
        measure(0).start()

        @pl.loop(0, chunks)
        def _(c):
            pl.when(c + 1 < chunks)(lambda: measure(c + 1).start())
            measure(c).wait()
            body(c)

    def second(c):
        arrive(lambda side: halo(ONCE, side, c))
        left(lambda side: halo(ONCE, side, c))
        left(lambda side: halo(START, side, c))
        each_wave(c, twice(c))
        send(lambda side: halo(FIRST, side, c))
        send(lambda side: halo(FLUENCE, side, c))
        stored(c).start()

    with_measured(second)

    def adjoint(c):
        def body(w, j):
            fill(FIRST, w, other)
            slot = lax.rem(c, 2)

            def tile(z, r, rows):
                absorb = absorption(spec, w, coef, z + 1, rows)
                a1, sv = around(vpad, z + 1, r, ROWS, masks)
                _, su = around(upad, z + 1, r, ROWS, masks)
                a2 = a1 + (half[w, z + 1, rows, :] * sv + su) * inverse[w, z, rows, :]
                other[w, z, rows, :] = a2
                f2 = field[w, z, rows, :]
                common = f2 * ((absorb * f2 - meas[slot, j, z, rows, :]) - a2)
                for chrom in range(4):
                    chroms[chrom, z, rows, :] += spec[w, chrom] * common

            each_tile(tile)

        return body

    def third(c):
        arrive(lambda side: halo(FIRST, side, c))
        left(lambda side: halo(FIRST, side, c))
        each_wave(c, adjoint(c))
        send(lambda side: halo(ADJOINT, side, c))

    with_measured(third)

    def share(k, part):
        return pltpu.make_async_remote_copy(
            src_ref=chroms if part == 0 else scats,
            dst_ref=partner.at[k, pl.ds(0, 4)] if part == 0 else partner.at[k, 4],
            send_sem=g_send.at[k, part],
            recv_sem=g_recv.at[k, part],
            device_id={"wl": lax.rem(mine + k + 1, peers + 1)},
            device_id_type=MESH,
        )

    for k in range(peers):
        share(k, 0).start()

    def scatter(w, _):
        fpad, apad = vpad, upad
        for z, side in ((0, 0), (nz + 1, 1)):
            fpad[z, mid, :] = halos[FLUENCE, side, w]
            apad[z, mid, :] = halos[ADJOINT, side, w]
            wpad[z, mid, :] = half[w, z]

        @pl.loop(0, nz)
        def _(z):
            fpad[z + 1, mid, :] = field[w, z]
            apad[z + 1, mid, :] = other[w, z]
            wpad[z + 1, mid, :] = half[w, z + 1]

        def tile(z, r, rows):
            f, fn = six(fpad, z + 1, r, ROWS, masks)
            a, an = six(apad, z + 1, r, ROWS, masks)
            h, hn = six(wpad, z + 1, r, ROWS, masks)
            coupling = jnp.zeros_like(f)
            for hs, fs, ls in zip(hn, fn, an):
                coupling = coupling + (h + hs) * ((fs - f) * (ls - a))
            scats[z, rows, :] += (12.0 * spec[w, 4]) * (h * h) * coupling

        each_tile(tile)

    @pl.loop(0, chunks)
    def _(c):
        arrive(lambda side: halo(FLUENCE, side, c))
        arrive(lambda side: halo(ADJOINT, side, c))
        each_wave(c, scatter)

    for k in range(peers):
        share(k, 1).start()

    @pl.loop(0, chunks)
    def _(c):
        left(lambda side: halo(FLUENCE, side, c))
        left(lambda side: halo(ADJOINT, side, c))
        stored(c).wait()

    left(tag)
    for k in range(peers):
        share(k, 0).wait()
        share(k, 1).wait()

    def plane(column, z):
        return chroms.at[column, z] if column < 4 else scats.at[z]

    sums[0] = jnp.zeros((5, 8, nx), jnp.float32)

    @pl.loop(0, nz)
    def _(z):
        for column in range(5):
            total = plane(column, z)[...]
            for k in range(peers):
                total = total + partner[k, column, z]
            plane(column, z)[...] = total
            sums[0, column] += jnp.sum((total * total).reshape(ny // 8, 8, nx), axis=0)

    def tell(step, k):
        return pltpu.make_async_remote_copy(
            src_ref=sums.at[step],
            dst_ref=sums_in.at[step, k - 1],
            send_sem=s_send.at[step, k - 1],
            recv_sem=s_recv.at[step, k - 1],
            device_id={"gz": fellow(step, k)},
            device_id_type=MESH,
        )

    for step, (_, radix) in enumerate(rounds):
        for k in range(1, radix):
            tell(step, k).start()
        total = sums[step]
        for k in range(1, radix):
            tell(step, k).wait()
            total = total + sums_in[step, k - 1]
        sums[step + 1] = total

    cells = nz * count * ny * nx
    rates = []
    for column in range(5):
        square = jnp.sum(sums[len(rounds), column], axis=(0, 1), keepdims=True)
        rates.append(-ETA / jnp.sqrt(square / cells + 1e-06))

    @pl.loop(0, nz)
    def _(z):
        for column in range(5):
            here = plane(column, z)
            here[...] = coef[column, z + 1] * jnp.exp(here[...] * rates[column])


def shards(labels, label_table, spectra, illumination, fluence_start, measured):
    waves, nz, ny, nx = fluence_start.shape
    per = 2 if waves % 2 == 0 else 1
    chunks = waves // per
    peers = lax.axis_size("wl") - 1
    slots = max(peers, 1)
    f32 = jnp.float32
    dma = pltpu.SemaphoreType.DMA
    smem = pl.BlockSpec(memory_space=SMEM)
    vmem = pl.BlockSpec(memory_space=pltpu.VMEM)
    anyspace = pl.BlockSpec(memory_space=pl.ANY)
    whole = pltpu.VMEM((waves, nz, ny, nx), f32)
    pad = pltpu.VMEM((nz + 2, ny + 2 * PAD, nx), f32)
    rounds = rounds_of(lax.axis_size("gz"))
    most = max([radix - 1 for _, radix in rounds] + [1])
    steps = max(len(rounds), 1)
    return pl.pallas_call(
        functools.partial(kernel, per),
        in_specs=[smem, smem, vmem, vmem, anyspace, anyspace],
        out_specs=[anyspace, vmem, vmem],
        out_shape=[
            jax.ShapeDtypeStruct((waves, nz, ny, nx), f32),
            jax.ShapeDtypeStruct((4, nz, ny, nx), f32),
            jax.ShapeDtypeStruct((nz, ny, nx), f32),
        ],
        scratch_shapes=[
            pltpu.VMEM((5, nz + 2, ny, nx), f32),
            whole,
            whole,
            pltpu.VMEM((waves, nz + 2, ny, nx), f32),
            whole,
            pltpu.VMEM((2, per, nz, ny, nx), f32),
            pltpu.VMEM((5, 2, waves, ny, nx), f32),
            pltpu.VMEM((2, ny, nx), jnp.int32),
            pad,
            pad,
            pad,
            pltpu.VMEM((slots, 5, nz, ny, nx), f32),
            pltpu.VMEM((steps + 1, 5, 8, nx), f32),
            pltpu.VMEM((steps, most, 5, 8, nx), f32),
            dma((5, 2, chunks)),
            dma((5, 2, chunks)),
            dma((2,)),
            dma((2,)),
            dma((chunks,)),
            dma((chunks,)),
            dma((2,)),
            dma((slots, 2)),
            dma((slots, 2)),
            dma((steps, most)),
            dma((steps, most)),
        ],
        cost_estimate=pl.CostEstimate(
            flops=waves * nz * ny * nx * 200,
            bytes_accessed=waves * nz * ny * nx * 16,
            transcendentals=0,
        ),
        compiler_params=pltpu.CompilerParams(
            collective_id=0, has_side_effects=True, vmem_limit_bytes=62 * 1024 * 1024
        ),
    )(spectra, label_table, labels, illumination, fluence_start, measured)


def solution(mesh):
    in_specs = (
        P("gz", None, None),
        P(),
        P("wl", None),
        P(),
        P("wl", "gz", None, None),
        P("wl", "gz", None, None),
    )
    out_specs = (P("wl", "gz", None, None), P(None, "gz", None, None), P("gz", None, None))
    return jax.shard_map(shards, mesh=mesh, in_specs=in_specs, out_specs=out_specs, check_vma=False)
```

```python
import functools

import jax
import jax.numpy as jnp
from jax import lax
from jax.experimental import pallas as pl
from jax.experimental.pallas import tpu as pltpu
from jax.sharding import PartitionSpec as P

ETA = 0.3
ROWS = 64
SLAB = 2
PAD = 8
SMEM = pltpu.SMEM
MESH = pl.DeviceIdType.MESH
START, ONCE, FLUENCE, FIRST, ADJOINT = range(5)


def edges(n, nx):
    lane = lax.broadcasted_iota(jnp.int32, (n, nx), 1)
    return lane < nx - 1, lane > 0


def six(pad, z, r, n, masks):
    nx = pad.shape[2]
    lo = PAD + r
    c = pad[z, lo : lo + n, :]
    xp = jnp.where(masks[0], pltpu.roll(c, nx - 1, 1), 0.0)
    xm = jnp.where(masks[1], pltpu.roll(c, 1, 1), 0.0)
    return c, (
        pad[z + 1, lo : lo + n, :],
        pad[z - 1, lo : lo + n, :],
        pad[z, lo + 1 : lo + n + 1, :],
        pad[z, lo - 1 : lo + n - 1, :],
        xp,
        xm,
    )


def around(pad, z, r, n, masks):
    c, nb = six(pad, z, r, n, masks)
    return c, ((nb[0] + nb[1]) + (nb[2] + nb[3])) + (nb[4] + nb[5])


def absorption(spec, w, coef, z, rows):
    total = spec[w, 0] * coef[0, z, rows, :]
    for chrom in range(1, 4):
        total = total + spec[w, chrom] * coef[chrom, z, rows, :]
    return total


def rounds_of(count):
    stride, rounds = 1, []
    while stride < count:
        rest = count // stride
        radix = 4 if rest % 4 == 0 else 2 if rest % 2 == 0 else rest
        rounds.append((stride, radix))
        stride *= radix
    return rounds


def kernel(
    per, spec, table, labels, illum, start, measured,
    f_out, chroms, scats,
    coef, field, other, half, inverse, meas, halos, tags, vpad, upad, wpad, partner, sums, sums_in,
    send_sem, recv_sem, tag_send, tag_recv, in_sem, out_sem, meas_sem, g_send, g_recv, s_send, s_recv,
):
    waves, nz, ny, nx = field.shape
    chunks = waves // per
    slab = SLAB if nz % SLAB == 0 else nz
    slabs = nz // slab
    peers = lax.axis_size("wl") - 1
    count = lax.axis_size("gz")
    idx = lax.axis_index("gz")
    has_lo, has_hi = idx > 0, idx < count - 1
    above, below = lax.rem(idx + 1, count), lax.rem(idx + count - 1, count)
    mine = lax.axis_index("wl")
    mid = slice(PAD, PAD + ny)
    masks = edges(ROWS, nx)

    barrier = pltpu.get_barrier_semaphore()

    def greet(axis, where):
        pl.semaphore_signal(barrier, inc=1, device_id={axis: where}, device_id_type=MESH)

    pl.when(has_hi)(lambda: greet("gz", above))
    pl.when(has_lo)(lambda: greet("gz", below))
    for k in range(peers):
        greet("wl", lax.rem(mine + k + 1, peers + 1))

    rounds = rounds_of(count)

    def fellow(step, k):
        stride, radix = rounds[step]
        digit = lax.rem(lax.div(idx, stride), radix)
        return idx + (lax.rem(digit + k, radix) - digit) * stride

    for step, (_, radix) in enumerate(rounds):
        for k in range(1, radix):
            greet("gz", fellow(step, k))
    met = peers + sum(radix - 1 for _, radix in rounds)

    def loaded(c):
        rows = pl.ds(c * per, per)
        return pltpu.make_async_copy(start.at[rows], field.at[rows], in_sem.at[c])

    def stored(c):
        rows = pl.ds(c * per, per)
        return pltpu.make_async_copy(field.at[rows], f_out.at[rows], out_sem.at[c])

    def measure(c):
        slot = lax.rem(c, 2)
        return pltpu.make_async_copy(
            measured.at[pl.ds(c * per, per)], meas.at[slot], meas_sem.at[slot]
        )

    @pl.loop(0, chunks)
    def _(c):
        loaded(c).start()

    def halo(kind, side, c):
        rows = pl.ds(c * per, per)
        plane = nz - 1 if side == 0 else 0
        source = {START: start, FLUENCE: field, ADJOINT: inverse}.get(kind, other)
        return pltpu.make_async_remote_copy(
            src_ref=source.at[rows, plane],
            dst_ref=halos.at[kind, side, rows],
            send_sem=send_sem.at[kind, side, c],
            recv_sem=recv_sem.at[kind, side, c],
            device_id={"gz": above if side == 0 else below},
            device_id_type=MESH,
        )

    def tag(side):
        return pltpu.make_async_remote_copy(
            src_ref=labels.at[nz - 1 if side == 0 else 0],
            dst_ref=tags.at[side],
            send_sem=tag_send.at[side],
            recv_sem=tag_recv.at[side],
            device_id={"gz": above if side == 0 else below},
            device_id_type=MESH,
        )

    def send(make):
        pl.when(has_hi)(lambda: make(0).start())
        pl.when(has_lo)(lambda: make(1).start())

    def arrive(make):
        pl.when(has_lo)(lambda: make(0).wait_recv())
        pl.when(has_hi)(lambda: make(1).wait_recv())

    def left(make):
        pl.when(has_hi)(lambda: make(0).wait_send())
        pl.when(has_lo)(lambda: make(1).wait_send())

    def blank(side):
        tags[side] = jnp.zeros((ny, nx), jnp.int32)

        @pl.loop(0, 5)
        def _(kind):
            @pl.loop(0, waves)
            def _(w):
                halos[kind, side, w] = jnp.zeros((ny, nx), jnp.float32)

    pl.when(jnp.logical_not(has_lo))(lambda: blank(0))
    pl.when(jnp.logical_not(has_hi))(lambda: blank(1))

    pl.semaphore_wait(barrier, has_lo.astype(jnp.int32) + has_hi.astype(jnp.int32) + met)

    send(tag)

    @pl.loop(0, chunks)
    def _(c):
        send(lambda side: halo(START, side, c))

    rim = jnp.zeros((nz + 2, PAD, nx), jnp.float32)
    for pad in (vpad, upad, wpad):
        pad[:, 0:PAD, :] = rim
        pad[:, PAD + ny : 2 * PAD + ny, :] = rim

    @pl.loop(0, nz)
    def _(z):
        chroms[:, z] = jnp.zeros((4, ny, nx), jnp.float32)
        scats[z] = jnp.zeros((ny, nx), jnp.float32)

    def lookup(z, classes):
        for r in range(0, ny, ROWS):
            tags_here = classes(slice(r, r + ROWS))
            same = [tags_here == k for k in range(1, table.shape[0])]
            for column in range(5):
                value = jnp.full((ROWS, nx), table[0, column], jnp.float32)
                for k, hit in enumerate(same):
                    value = jnp.where(hit, table[k + 1, column], value)
                coef[column, z, r : r + ROWS, :] = value

    @pl.loop(0, nz)
    def _(z):
        lookup(z + 1, lambda rows: labels[z, rows, :])

    arrive(tag)
    lookup(0, lambda rows: tags[0, rows, :])
    lookup(nz + 1, lambda rows: tags[1, rows, :])

    lo_flag, hi_flag = has_lo.astype(jnp.float32), has_hi.astype(jnp.float32)

    def each_wave(c, body):
        @pl.loop(0, per)
        def _(j):
            body(c * per + j, j)

    def each_tile(body):
        @pl.loop(0, nz)
        def _(z):
            for r in range(0, ny, ROWS):
                body(z, r, slice(r, r + ROWS))

    def fill(kind, w, values):
        def put(z, v):
            vpad[z, mid, :] = v
            upad[z, mid, :] = v * half[w, z]

        put(0, halos[kind, 0, w])
        put(nz + 1, halos[kind, 1, w])

        @pl.loop(0, nz)
        def _(z):
            put(z + 1, values[w, z])

    def once(w, _):
        def optics(z, flag, v):
            for r in range(0, ny, ROWS):
                rows = slice(r, r + ROWS)
                here = slice(PAD + r, PAD + r + ROWS)
                absorb = absorption(spec, w, coef, z, rows)
                h = 1.0 / (6.0 * (absorb + spec[w, 4] * coef[4, z, rows, :]))
                if flag is not None:
                    h = h * flag
                value = v(rows)
                half[w, z, rows, :] = h
                wpad[z, here, :] = h
                vpad[z, here, :] = value
                upad[z, here, :] = value * h

        optics(0, lo_flag, lambda rows: halos[START, 0, w, rows, :])
        optics(nz + 1, hi_flag, lambda rows: halos[START, 1, w, rows, :])

        @pl.loop(0, nz)
        def _(z):
            optics(z + 1, None, lambda rows: field[w, z, rows, :])

        def tile(z, r, rows):
            absorb = absorption(spec, w, coef, z + 1, rows)
            h, sh = around(wpad, z + 1, r, ROWS, masks)
            t = 1.0 / (absorb + 6.0 * h + sh)
            _, sv = around(vpad, z + 1, r, ROWS, masks)
            _, su = around(upad, z + 1, r, ROWS, masks)
            source = spec[w, 5] * illum[rows, :].astype(jnp.float32)
            inverse[w, z, rows, :] = t
            other[w, z, rows, :] = (source + h * sv + su) * t

        each_tile(tile)

    @pl.loop(0, chunks)
    def _(c):
        loaded(c).wait()
        arrive(lambda side: halo(START, side, c))
        each_wave(c, once)
        send(lambda side: halo(ONCE, side, c))

    def twice(c):
        def body(w, j):
            fill(ONCE, w, other)
            slot = lax.rem(c, 2)

            def tile(z, r, rows):
                absorb = absorption(spec, w, coef, z + 1, rows)
                _, sv = around(vpad, z + 1, r, ROWS, masks)
                _, su = around(upad, z + 1, r, ROWS, masks)
                t = inverse[w, z, rows, :]
                source = spec[w, 5] * illum[rows, :].astype(jnp.float32)
                f2 = (source + half[w, z + 1, rows, :] * sv + su) * t
                field[w, z, rows, :] = f2
                other[w, z, rows, :] = absorb * (absorb * f2 - meas[slot, j, z, rows, :]) * t

            each_tile(tile)

        return body

    def with_measured(body):
        measure(0).start()

        @pl.loop(0, chunks)
        def _(c):
            pl.when(c + 1 < chunks)(lambda: measure(c + 1).start())
            measure(c).wait()
            body(c)

    def second(c):
        arrive(lambda side: halo(ONCE, side, c))
        left(lambda side: halo(ONCE, side, c))
        left(lambda side: halo(START, side, c))
        each_wave(c, twice(c))
        send(lambda side: halo(FIRST, side, c))
        send(lambda side: halo(FLUENCE, side, c))
        stored(c).start()

    with_measured(second)

    def adjoint(c, z0):
        def body(w, j):
            def put(p, v):
                vpad[p, mid, :] = v
                upad[p, mid, :] = v * half[w, z0 + p]

            put(0, halos[FIRST, 0, w] if z0 == 0 else other[w, z0 - 1])
            for p in range(1, slab + 1):
                put(p, other[w, z0 + p - 1])
            put(slab + 1, halos[FIRST, 1, w] if z0 + slab == nz else other[w, z0 + slab])
            slot = lax.rem(c, 2)

            @pl.loop(0, slab)
            def _(p):
                z = z0 + p
                for r in range(0, ny, ROWS):
                    rows = slice(r, r + ROWS)
                    absorb = absorption(spec, w, coef, z + 1, rows)
                    a1, sv = around(vpad, p + 1, r, ROWS, masks)
                    _, su = around(upad, p + 1, r, ROWS, masks)
                    a2 = a1 + (half[w, z + 1, rows, :] * sv + su) * inverse[w, z, rows, :]
                    inverse[w, z, rows, :] = a2
                    f2 = field[w, z, rows, :]
                    common = f2 * ((absorb * f2 - meas[slot, j, p, rows, :]) - a2)
                    for chrom in range(4):
                        chroms[chrom, z, rows, :] += spec[w, chrom] * common

        return body

    def third(z0):
        def measure_slab(c):
            slot = lax.rem(c, 2)
            return pltpu.make_async_copy(
                measured.at[pl.ds(c * per, per), pl.ds(z0, slab)],
                meas.at[slot, :, pl.ds(0, slab)],
                meas_sem.at[slot],
            )

        measure_slab(0).start()

        @pl.loop(0, chunks)
        def _(c):
            pl.when(c + 1 < chunks)(lambda: measure_slab(c + 1).start())
            measure_slab(c).wait()
            if z0 == 0:
                pl.when(has_lo)(lambda: halo(FIRST, 0, c).wait_recv())
            if z0 + slab == nz:
                pl.when(has_hi)(lambda: halo(FIRST, 1, c).wait_recv())
            each_wave(c, adjoint(c, z0))
            if z0 == 0:
                pl.when(has_lo)(lambda: halo(ADJOINT, 1, c).start())
            if z0 + slab == nz:
                pl.when(has_hi)(lambda: halo(ADJOINT, 0, c).start())

    def share(k, part):
        planes = pl.ds(part * slab, slab)
        last = part == slabs
        return pltpu.make_async_remote_copy(
            src_ref=scats if last else chroms.at[:, planes],
            dst_ref=partner.at[k, 4] if last else partner.at[k, pl.ds(0, 4), planes],
            send_sem=g_send.at[k, part],
            recv_sem=g_recv.at[k, part],
            device_id={"wl": lax.rem(mine + k + 1, peers + 1)},
            device_id_type=MESH,
        )

    inner = list(range(1, slabs - 1))
    for part in inner[:1] + sorted({0, slabs - 1}) + inner[1:]:
        third(part * slab)
        for k in range(peers):
            share(k, part).start()

    def scatter(w, _):
        fpad, apad = vpad, upad
        for z, side in ((0, 0), (nz + 1, 1)):
            fpad[z, mid, :] = halos[FLUENCE, side, w]
            apad[z, mid, :] = halos[ADJOINT, side, w]
            wpad[z, mid, :] = half[w, z]

        @pl.loop(0, nz)
        def _(z):
            fpad[z + 1, mid, :] = field[w, z]
            apad[z + 1, mid, :] = inverse[w, z]
            wpad[z + 1, mid, :] = half[w, z + 1]

        def tile(z, r, rows):
            f, fn = six(fpad, z + 1, r, ROWS, masks)
            a, an = six(apad, z + 1, r, ROWS, masks)
            h, hn = six(wpad, z + 1, r, ROWS, masks)
            coupling = jnp.zeros_like(f)
            for hs, fs, ls in zip(hn, fn, an):
                coupling = coupling + (h + hs) * ((fs - f) * (ls - a))
            scats[z, rows, :] += (12.0 * spec[w, 4]) * (h * h) * coupling

        each_tile(tile)

    @pl.loop(0, chunks)
    def _(c):
        arrive(lambda side: halo(FLUENCE, side, c))
        arrive(lambda side: halo(ADJOINT, side, c))
        each_wave(c, scatter)

    for k in range(peers):
        share(k, slabs).start()

    @pl.loop(0, chunks)
    def _(c):
        left(lambda side: halo(FIRST, side, c))
        left(lambda side: halo(FLUENCE, side, c))
        left(lambda side: halo(ADJOINT, side, c))
        stored(c).wait()

    left(tag)
    for k in range(peers):
        for part in range(slabs + 1):
            share(k, part).wait()

    def plane(column, z):
        return chroms.at[column, z] if column < 4 else scats.at[z]

    sums[0] = jnp.zeros((5, 8, nx), jnp.float32)

    @pl.loop(0, nz)
    def _(z):
        for column in range(5):
            total = plane(column, z)[...]
            for k in range(peers):
                total = total + partner[k, column, z]
            plane(column, z)[...] = total
            sums[0, column] += jnp.sum((total * total).reshape(ny // 8, 8, nx), axis=0)

    def tell(step, k):
        return pltpu.make_async_remote_copy(
            src_ref=sums.at[step],
            dst_ref=sums_in.at[step, k - 1],
            send_sem=s_send.at[step, k - 1],
            recv_sem=s_recv.at[step, k - 1],
            device_id={"gz": fellow(step, k)},
            device_id_type=MESH,
        )

    for step, (_, radix) in enumerate(rounds):
        for k in range(1, radix):
            tell(step, k).start()
        total = sums[step]
        for k in range(1, radix):
            tell(step, k).wait()
            total = total + sums_in[step, k - 1]
        sums[step + 1] = total

    cells = nz * count * ny * nx
    rates = []
    for column in range(5):
        square = jnp.sum(sums[len(rounds), column], axis=(0, 1), keepdims=True)
        rates.append(-ETA / jnp.sqrt(square / cells + 1e-06))

    @pl.loop(0, nz)
    def _(z):
        for column in range(5):
            here = plane(column, z)
            here[...] = coef[column, z + 1] * jnp.exp(here[...] * rates[column])


def shards(labels, label_table, spectra, illumination, fluence_start, measured):
    waves, nz, ny, nx = fluence_start.shape
    per = 2 if waves % 2 == 0 else 1
    chunks = waves // per
    peers = lax.axis_size("wl") - 1
    slots = max(peers, 1)
    f32 = jnp.float32
    dma = pltpu.SemaphoreType.DMA
    smem = pl.BlockSpec(memory_space=SMEM)
    vmem = pl.BlockSpec(memory_space=pltpu.VMEM)
    anyspace = pl.BlockSpec(memory_space=pl.ANY)
    whole = pltpu.VMEM((waves, nz, ny, nx), f32)
    pad = pltpu.VMEM((nz + 2, ny + 2 * PAD, nx), f32)
    rounds = rounds_of(lax.axis_size("gz"))
    most = max([radix - 1 for _, radix in rounds] + [1])
    steps = max(len(rounds), 1)
    return pl.pallas_call(
        functools.partial(kernel, per),
        in_specs=[smem, smem, vmem, vmem, anyspace, anyspace],
        out_specs=[anyspace, vmem, vmem],
        out_shape=[
            jax.ShapeDtypeStruct((waves, nz, ny, nx), f32),
            jax.ShapeDtypeStruct((4, nz, ny, nx), f32),
            jax.ShapeDtypeStruct((nz, ny, nx), f32),
        ],
        scratch_shapes=[
            pltpu.VMEM((5, nz + 2, ny, nx), f32),
            whole,
            whole,
            pltpu.VMEM((waves, nz + 2, ny, nx), f32),
            whole,
            pltpu.VMEM((2, per, nz, ny, nx), f32),
            pltpu.VMEM((5, 2, waves, ny, nx), f32),
            pltpu.VMEM((2, ny, nx), jnp.int32),
            pad,
            pad,
            pad,
            pltpu.VMEM((slots, 5, nz, ny, nx), f32),
            pltpu.VMEM((steps + 1, 5, 8, nx), f32),
            pltpu.VMEM((steps, most, 5, 8, nx), f32),
            dma((5, 2, chunks)),
            dma((5, 2, chunks)),
            dma((2,)),
            dma((2,)),
            dma((chunks,)),
            dma((chunks,)),
            dma((2,)),
            dma((slots, nz + 1)),
            dma((slots, nz + 1)),
            dma((steps, most)),
            dma((steps, most)),
        ],
        cost_estimate=pl.CostEstimate(
            flops=waves * nz * ny * nx * 200,
            bytes_accessed=waves * nz * ny * nx * 16,
            transcendentals=0,
        ),
        compiler_params=pltpu.CompilerParams(
            collective_id=0, has_side_effects=True, vmem_limit_bytes=62 * 1024 * 1024
        ),
    )(spectra, label_table, labels, illumination, fluence_start, measured)


def solution(mesh):
    in_specs = (
        P("gz", None, None),
        P(),
        P("wl", None),
        P(),
        P("wl", "gz", None, None),
        P("wl", "gz", None, None),
    )
    out_specs = (P("wl", "gz", None, None), P(None, "gz", None, None), P("gz", None, None))
    return jax.shard_map(shards, mesh=mesh, in_specs=in_specs, out_specs=out_specs, check_vma=False)
```

```python
import functools

import jax
import jax.numpy as jnp
from jax import lax
from jax.experimental import pallas as pl
from jax.experimental.pallas import tpu as pltpu
from jax.sharding import PartitionSpec as P

ETA = 0.3
ROWS = 64
SLAB = 4
PAD = 8
SMEM = pltpu.SMEM
MESH = pl.DeviceIdType.MESH
START, ONCE, FLUENCE, FIRST, ADJOINT = range(5)


def edges(n, nx):
    lane = lax.broadcasted_iota(jnp.int32, (n, nx), 1)
    return lane < nx - 1, lane > 0


def six(pad, z, r, n, masks):
    nx = pad.shape[2]
    lo = PAD + r
    c = pad[z, lo : lo + n, :]
    xp = jnp.where(masks[0], pltpu.roll(c, nx - 1, 1), 0.0)
    xm = jnp.where(masks[1], pltpu.roll(c, 1, 1), 0.0)
    return c, (
        pad[z + 1, lo : lo + n, :],
        pad[z - 1, lo : lo + n, :],
        pad[z, lo + 1 : lo + n + 1, :],
        pad[z, lo - 1 : lo + n - 1, :],
        xp,
        xm,
    )


def around(pad, z, r, n, masks):
    c, nb = six(pad, z, r, n, masks)
    return c, ((nb[0] + nb[1]) + (nb[2] + nb[3])) + (nb[4] + nb[5])


def absorption(spec, w, coef, z, rows):
    total = spec[w, 0] * coef[0, z, rows, :]
    for chrom in range(1, 4):
        total = total + spec[w, chrom] * coef[chrom, z, rows, :]
    return total


def rounds_of(count):
    stride, rounds = 1, []
    while stride < count:
        rest = count // stride
        radix = 4 if rest % 4 == 0 else 2 if rest % 2 == 0 else rest
        rounds.append((stride, radix))
        stride *= radix
    return rounds


def kernel(
    per, spec, table, labels, illum, start, measured,
    f_out, chroms, scats,
    coef, field, other, half, inverse, meas, halos, tags, vpad, upad, wpad, partner, sums, sums_in,
    send_sem, recv_sem, tag_send, tag_recv, in_sem, out_sem, meas_sem, g_send, g_recv, s_send, s_recv,
):
    waves, nz, ny, nx = field.shape
    chunks = waves // per
    slab = SLAB if nz % SLAB == 0 else nz
    slabs = nz // slab
    peers = lax.axis_size("wl") - 1
    count = lax.axis_size("gz")
    idx = lax.axis_index("gz")
    has_lo, has_hi = idx > 0, idx < count - 1
    above, below = lax.rem(idx + 1, count), lax.rem(idx + count - 1, count)
    mine = lax.axis_index("wl")
    mid = slice(PAD, PAD + ny)
    masks = edges(ROWS, nx)

    barrier = pltpu.get_barrier_semaphore()

    def greet(axis, where):
        pl.semaphore_signal(barrier, inc=1, device_id={axis: where}, device_id_type=MESH)

    pl.when(has_hi)(lambda: greet("gz", above))
    pl.when(has_lo)(lambda: greet("gz", below))
    for k in range(peers):
        greet("wl", lax.rem(mine + k + 1, peers + 1))

    rounds = rounds_of(count)

    def fellow(step, k):
        stride, radix = rounds[step]
        digit = lax.rem(lax.div(idx, stride), radix)
        return idx + (lax.rem(digit + k, radix) - digit) * stride

    for step, (_, radix) in enumerate(rounds):
        for k in range(1, radix):
            greet("gz", fellow(step, k))
    met = peers + sum(radix - 1 for _, radix in rounds)

    def loaded(c):
        rows = pl.ds(c * per, per)
        return pltpu.make_async_copy(start.at[rows], field.at[rows], in_sem.at[c])

    def stored(c):
        rows = pl.ds(c * per, per)
        return pltpu.make_async_copy(field.at[rows], f_out.at[rows], out_sem.at[c])

    def measure(c):
        slot = lax.rem(c, 2)
        return pltpu.make_async_copy(
            measured.at[pl.ds(c * per, per)], meas.at[slot], meas_sem.at[slot]
        )

    @pl.loop(0, chunks)
    def _(c):
        loaded(c).start()

    def halo(kind, side, c):
        rows = pl.ds(c * per, per)
        plane = nz - 1 if side == 0 else 0
        source = {START: start, FLUENCE: field, ADJOINT: inverse}.get(kind, other)
        return pltpu.make_async_remote_copy(
            src_ref=source.at[rows, plane],
            dst_ref=halos.at[kind, side, rows],
            send_sem=send_sem.at[kind, side, c],
            recv_sem=recv_sem.at[kind, side, c],
            device_id={"gz": above if side == 0 else below},
            device_id_type=MESH,
        )

    def tag(side):
        return pltpu.make_async_remote_copy(
            src_ref=labels.at[nz - 1 if side == 0 else 0],
            dst_ref=tags.at[side],
            send_sem=tag_send.at[side],
            recv_sem=tag_recv.at[side],
            device_id={"gz": above if side == 0 else below},
            device_id_type=MESH,
        )

    def send(make):
        pl.when(has_hi)(lambda: make(0).start())
        pl.when(has_lo)(lambda: make(1).start())

    def arrive(make):
        pl.when(has_lo)(lambda: make(0).wait_recv())
        pl.when(has_hi)(lambda: make(1).wait_recv())

    def left(make):
        pl.when(has_hi)(lambda: make(0).wait_send())
        pl.when(has_lo)(lambda: make(1).wait_send())

    def blank(side):
        tags[side] = jnp.zeros((ny, nx), jnp.int32)

        @pl.loop(0, 5)
        def _(kind):
            @pl.loop(0, waves)
            def _(w):
                halos[kind, side, w] = jnp.zeros((ny, nx), jnp.float32)

    pl.when(jnp.logical_not(has_lo))(lambda: blank(0))
    pl.when(jnp.logical_not(has_hi))(lambda: blank(1))

    pl.semaphore_wait(barrier, has_lo.astype(jnp.int32) + has_hi.astype(jnp.int32) + met)

    send(tag)

    @pl.loop(0, chunks)
    def _(c):
        send(lambda side: halo(START, side, c))

    rim = jnp.zeros((nz + 2, PAD, nx), jnp.float32)
    for pad in (vpad, upad, wpad):
        pad[:, 0:PAD, :] = rim
        pad[:, PAD + ny : 2 * PAD + ny, :] = rim

    @pl.loop(0, nz)
    def _(z):
        chroms[:, z] = jnp.zeros((4, ny, nx), jnp.float32)
        scats[z] = jnp.zeros((ny, nx), jnp.float32)

    def lookup(z, classes):
        for r in range(0, ny, ROWS):
            tags_here = classes(slice(r, r + ROWS))
            same = [tags_here == k for k in range(1, table.shape[0])]
            for column in range(5):
                value = jnp.full((ROWS, nx), table[0, column], jnp.float32)
                for k, hit in enumerate(same):
                    value = jnp.where(hit, table[k + 1, column], value)
                coef[column, z, r : r + ROWS, :] = value

    @pl.loop(0, nz)
    def _(z):
        lookup(z + 1, lambda rows: labels[z, rows, :])

    arrive(tag)
    lookup(0, lambda rows: tags[0, rows, :])
    lookup(nz + 1, lambda rows: tags[1, rows, :])

    lo_flag, hi_flag = has_lo.astype(jnp.float32), has_hi.astype(jnp.float32)

    def each_wave(c, body):
        @pl.loop(0, per)
        def _(j):
            body(c * per + j, j)

    def each_tile(body):
        @pl.loop(0, nz)
        def _(z):
            for r in range(0, ny, ROWS):
                body(z, r, slice(r, r + ROWS))

    def fill(kind, w, values):
        def put(z, v):
            vpad[z, mid, :] = v
            upad[z, mid, :] = v * half[w, z]

        put(0, halos[kind, 0, w])
        put(nz + 1, halos[kind, 1, w])

        @pl.loop(0, nz)
        def _(z):
            put(z + 1, values[w, z])

    def once(w, _):
        def optics(z, flag, v):
            for r in range(0, ny, ROWS):
                rows = slice(r, r + ROWS)
                here = slice(PAD + r, PAD + r + ROWS)
                absorb = absorption(spec, w, coef, z, rows)
                h = 1.0 / (6.0 * (absorb + spec[w, 4] * coef[4, z, rows, :]))
                if flag is not None:
                    h = h * flag
                value = v(rows)
                half[w, z, rows, :] = h
                wpad[z, here, :] = h
                vpad[z, here, :] = value
                upad[z, here, :] = value * h

        optics(0, lo_flag, lambda rows: halos[START, 0, w, rows, :])
        optics(nz + 1, hi_flag, lambda rows: halos[START, 1, w, rows, :])

        @pl.loop(0, nz)
        def _(z):
            optics(z + 1, None, lambda rows: field[w, z, rows, :])

        def tile(z, r, rows):
            absorb = absorption(spec, w, coef, z + 1, rows)
            h, sh = around(wpad, z + 1, r, ROWS, masks)
            t = 1.0 / (absorb + 6.0 * h + sh)
            _, sv = around(vpad, z + 1, r, ROWS, masks)
            _, su = around(upad, z + 1, r, ROWS, masks)
            source = spec[w, 5] * illum[rows, :].astype(jnp.float32)
            inverse[w, z, rows, :] = t
            other[w, z, rows, :] = (source + h * sv + su) * t

        each_tile(tile)

    @pl.loop(0, chunks)
    def _(c):
        loaded(c).wait()
        arrive(lambda side: halo(START, side, c))
        each_wave(c, once)
        send(lambda side: halo(ONCE, side, c))

    def twice(c):
        def body(w, j):
            fill(ONCE, w, other)
            slot = lax.rem(c, 2)

            def tile(z, r, rows):
                absorb = absorption(spec, w, coef, z + 1, rows)
                _, sv = around(vpad, z + 1, r, ROWS, masks)
                _, su = around(upad, z + 1, r, ROWS, masks)
                t = inverse[w, z, rows, :]
                source = spec[w, 5] * illum[rows, :].astype(jnp.float32)
                f2 = (source + half[w, z + 1, rows, :] * sv + su) * t
                field[w, z, rows, :] = f2
                other[w, z, rows, :] = absorb * (absorb * f2 - meas[slot, j, z, rows, :]) * t

            each_tile(tile)

        return body

    def with_measured(body):
        measure(0).start()

        @pl.loop(0, chunks)
        def _(c):
            pl.when(c + 1 < chunks)(lambda: measure(c + 1).start())
            measure(c).wait()
            body(c)

    def second(c):
        arrive(lambda side: halo(ONCE, side, c))
        left(lambda side: halo(ONCE, side, c))
        left(lambda side: halo(START, side, c))
        each_wave(c, twice(c))
        send(lambda side: halo(FIRST, side, c))
        stored(c).start()

    with_measured(second)

    def adjoint(c, z0):
        def body(w, j):
            def put(p, v):
                vpad[p, mid, :] = v
                upad[p, mid, :] = v * half[w, z0 + p]

            put(0, halos[FIRST, 0, w] if z0 == 0 else other[w, z0 - 1])
            for p in range(1, slab + 1):
                put(p, other[w, z0 + p - 1])
            put(slab + 1, halos[FIRST, 1, w] if z0 + slab == nz else other[w, z0 + slab])
            slot = lax.rem(c, 2)

            @pl.loop(0, slab)
            def _(p):
                z = z0 + p
                for r in range(0, ny, ROWS):
                    rows = slice(r, r + ROWS)
                    absorb = absorption(spec, w, coef, z + 1, rows)
                    a1, sv = around(vpad, p + 1, r, ROWS, masks)
                    _, su = around(upad, p + 1, r, ROWS, masks)
                    a2 = a1 + (half[w, z + 1, rows, :] * sv + su) * inverse[w, z, rows, :]
                    inverse[w, z, rows, :] = a2
                    f2 = field[w, z, rows, :]
                    common = f2 * ((absorb * f2 - meas[slot, j, p, rows, :]) - a2)
                    for chrom in range(4):
                        chroms[chrom, z, rows, :] += spec[w, chrom] * common

        return body

    def third(z0, first):
        def measure_slab(c):
            slot = lax.rem(c, 2)
            return pltpu.make_async_copy(
                measured.at[pl.ds(c * per, per), pl.ds(z0, slab)],
                meas.at[slot, :, pl.ds(0, slab)],
                meas_sem.at[slot],
            )

        measure_slab(0).start()

        @pl.loop(0, chunks)
        def _(c):
            pl.when(c + 1 < chunks)(lambda: measure_slab(c + 1).start())
            measure_slab(c).wait()
            if first:
                send(lambda side: halo(FLUENCE, side, c))
            if z0 == 0:
                pl.when(has_lo)(lambda: halo(FIRST, 0, c).wait_recv())
            if z0 + slab == nz:
                pl.when(has_hi)(lambda: halo(FIRST, 1, c).wait_recv())
            each_wave(c, adjoint(c, z0))
            if z0 == 0:
                pl.when(has_lo)(lambda: halo(ADJOINT, 1, c).start())
            if z0 + slab == nz:
                pl.when(has_hi)(lambda: halo(ADJOINT, 0, c).start())

    def share(k, part):
        planes = pl.ds(part * slab, slab)
        last = part == slabs
        return pltpu.make_async_remote_copy(
            src_ref=scats if last else chroms.at[:, planes],
            dst_ref=partner.at[k, 4] if last else partner.at[k, pl.ds(0, 4), planes],
            send_sem=g_send.at[k, part],
            recv_sem=g_recv.at[k, part],
            device_id={"wl": lax.rem(mine + k + 1, peers + 1)},
            device_id_type=MESH,
        )

    inner = list(range(1, slabs - 1))
    for turn, part in enumerate(inner[:1] + sorted({0, slabs - 1}) + inner[1:]):
        third(part * slab, turn == 0)
        for k in range(peers):
            share(k, part).start()

    def scatter(w, _):
        fpad, apad = vpad, upad
        for z, side in ((0, 0), (nz + 1, 1)):
            fpad[z, mid, :] = halos[FLUENCE, side, w]
            apad[z, mid, :] = halos[ADJOINT, side, w]
            wpad[z, mid, :] = half[w, z]

        @pl.loop(0, nz)
        def _(z):
            fpad[z + 1, mid, :] = field[w, z]
            apad[z + 1, mid, :] = inverse[w, z]
            wpad[z + 1, mid, :] = half[w, z + 1]

        def tile(z, r, rows):
            f, fn = six(fpad, z + 1, r, ROWS, masks)
            a, an = six(apad, z + 1, r, ROWS, masks)
            h, hn = six(wpad, z + 1, r, ROWS, masks)
            coupling = jnp.zeros_like(f)
            for hs, fs, ls in zip(hn, fn, an):
                coupling = coupling + (h + hs) * ((fs - f) * (ls - a))
            scats[z, rows, :] += (12.0 * spec[w, 4]) * (h * h) * coupling

        each_tile(tile)

    @pl.loop(0, chunks)
    def _(c):
        arrive(lambda side: halo(FLUENCE, side, c))
        arrive(lambda side: halo(ADJOINT, side, c))
        each_wave(c, scatter)

    for k in range(peers):
        share(k, slabs).start()

    @pl.loop(0, chunks)
    def _(c):
        left(lambda side: halo(FIRST, side, c))
        left(lambda side: halo(FLUENCE, side, c))
        left(lambda side: halo(ADJOINT, side, c))
        stored(c).wait()

    left(tag)
    for k in range(peers):
        for part in range(slabs + 1):
            share(k, part).wait()

    def plane(column, z):
        return chroms.at[column, z] if column < 4 else scats.at[z]

    sums[0] = jnp.zeros((5, 8, nx), jnp.float32)

    @pl.loop(0, nz)
    def _(z):
        for column in range(5):
            total = plane(column, z)[...]
            for k in range(peers):
                total = total + partner[k, column, z]
            plane(column, z)[...] = total
            sums[0, column] += jnp.sum((total * total).reshape(ny // 8, 8, nx), axis=0)

    def tell(step, k):
        return pltpu.make_async_remote_copy(
            src_ref=sums.at[step],
            dst_ref=sums_in.at[step, k - 1],
            send_sem=s_send.at[step, k - 1],
            recv_sem=s_recv.at[step, k - 1],
            device_id={"gz": fellow(step, k)},
            device_id_type=MESH,
        )

    for step, (_, radix) in enumerate(rounds):
        for k in range(1, radix):
            tell(step, k).start()
        total = sums[step]
        for k in range(1, radix):
            tell(step, k).wait()
            total = total + sums_in[step, k - 1]
        sums[step + 1] = total

    cells = nz * count * ny * nx
    rates = []
    for column in range(5):
        square = jnp.sum(sums[len(rounds), column], axis=(0, 1), keepdims=True)
        rates.append(-ETA / jnp.sqrt(square / cells + 1e-06))

    @pl.loop(0, nz)
    def _(z):
        for column in range(5):
            here = plane(column, z)
            here[...] = coef[column, z + 1] * jnp.exp(here[...] * rates[column])


def shards(labels, label_table, spectra, illumination, fluence_start, measured):
    waves, nz, ny, nx = fluence_start.shape
    per = 2 if waves % 2 == 0 else 1
    chunks = waves // per
    peers = lax.axis_size("wl") - 1
    slots = max(peers, 1)
    f32 = jnp.float32
    dma = pltpu.SemaphoreType.DMA
    smem = pl.BlockSpec(memory_space=SMEM)
    vmem = pl.BlockSpec(memory_space=pltpu.VMEM)
    anyspace = pl.BlockSpec(memory_space=pl.ANY)
    whole = pltpu.VMEM((waves, nz, ny, nx), f32)
    pad = pltpu.VMEM((nz + 2, ny + 2 * PAD, nx), f32)
    rounds = rounds_of(lax.axis_size("gz"))
    most = max([radix - 1 for _, radix in rounds] + [1])
    steps = max(len(rounds), 1)
    return pl.pallas_call(
        functools.partial(kernel, per),
        in_specs=[smem, smem, vmem, vmem, anyspace, anyspace],
        out_specs=[anyspace, vmem, vmem],
        out_shape=[
            jax.ShapeDtypeStruct((waves, nz, ny, nx), f32),
            jax.ShapeDtypeStruct((4, nz, ny, nx), f32),
            jax.ShapeDtypeStruct((nz, ny, nx), f32),
        ],
        scratch_shapes=[
            pltpu.VMEM((5, nz + 2, ny, nx), f32),
            whole,
            whole,
            pltpu.VMEM((waves, nz + 2, ny, nx), f32),
            whole,
            pltpu.VMEM((2, per, nz, ny, nx), f32),
            pltpu.VMEM((5, 2, waves, ny, nx), f32),
            pltpu.VMEM((2, ny, nx), jnp.int32),
            pad,
            pad,
            pad,
            pltpu.VMEM((slots, 5, nz, ny, nx), f32),
            pltpu.VMEM((steps + 1, 5, 8, nx), f32),
            pltpu.VMEM((steps, most, 5, 8, nx), f32),
            dma((5, 2, chunks)),
            dma((5, 2, chunks)),
            dma((2,)),
            dma((2,)),
            dma((chunks,)),
            dma((chunks,)),
            dma((2,)),
            dma((slots, nz + 1)),
            dma((slots, nz + 1)),
            dma((steps, most)),
            dma((steps, most)),
        ],
        cost_estimate=pl.CostEstimate(
            flops=waves * nz * ny * nx * 200,
            bytes_accessed=waves * nz * ny * nx * 16,
            transcendentals=0,
        ),
        compiler_params=pltpu.CompilerParams(
            collective_id=0, has_side_effects=True, vmem_limit_bytes=62 * 1024 * 1024
        ),
    )(spectra, label_table, labels, illumination, fluence_start, measured)


def solution(mesh):
    in_specs = (
        P("gz", None, None),
        P(),
        P("wl", None),
        P(),
        P("wl", "gz", None, None),
        P("wl", "gz", None, None),
    )
    out_specs = (P("wl", "gz", None, None), P(None, "gz", None, None), P("gz", None, None))
    return jax.shard_map(shards, mesh=mesh, in_specs=in_specs, out_specs=out_specs, check_vma=False)
```
